32 devices in a mesh: grp: 2 (over x), chan: 16 (over z, y, core).
Axes of the slice: x: 2, y: 2, z: 4, core: 2. Of those that a mesh axis runs over, the one named last changes fastest.
Arguments:
- samples: bfloat16 [32, 16, 256, 1024], P(('grp', 'chan')), parts along dimension 0, may hold values from -6 to 6
- fir: float32 [16, 1024], replicated, may hold values from -1.5 to 1.5
- chan_assign: int32 [256], replicated, may hold values from 0 to 511, as said below
- input_order: int32 [1024], replicated, may hold values from 0 to 1023, each once
Outputs:
- vis: bfloat16 [512, 1024, 1024], P(('grp', 'chan')), parts along dimension 0
The draws below stay inside these ranges and needn't reach their ends.
There are 2 independent parts, one for each index of `grp`. The reference program is written for one: setup_inputs(seed, part) draws one part's arguments, and reference() takes and returns one part's arrays. A program takes and returns all parts, laid end to end along the dimension named above; an argument that names none is the same for every part. Nothing has to cross between parts.
Inputs may be any that keep to these rules, and one draw needn't show every extreme that they name: `chan_assign`: distinct transform bins; bin 0 and bin 1024 // 2 - 1 are always among them. `input_order`: each input number once.
All inputs are finite; a program needn't handle non-finite values.
Results may differ from the reference program's by a relative error of at most 0.0074.
Values may be sent and summed in bfloat16 or wider, within the bound.
A program may use at most 256 MiB of HBM per device.

```python
import math
import jax
import jax.numpy as jnp
from jax import lax

INPUTS = 1024
FRAME = 1024
NCH = 256
TAPS = 16
QUART = 4
FQ = 16
SPECTRA = 64
AGROUPS = 4
IN_DEV = 256


def draw_chan_assign(key, part):
    key_middle = jax.random.fold_in(key, 11)
    key_mixing = jax.random.fold_in(key, 12)
    middle = jax.random.permutation(key_middle, FRAME // 2 - 2)[:NCH - 2].astype(jnp.int32) + 1
    ends = jnp.array([0, FRAME // 2 - 1], dtype=jnp.int32)
    values = jnp.concatenate([ends, middle])
    return jax.random.permutation(key_mixing, values).astype(jnp.int32)


def levels(rng, extent, cuts, least, high):
    gain = 1.0
    for position, parts in cuts:
        steps = jax.random.uniform(jax.random.fold_in(jax.random.fold_in(rng, 6), position), (parts,), jnp.float32, least / len(cuts), high / len(cuts))
        gain = gain * jnp.repeat(jnp.exp(steps), extent[position] // parts).reshape((-1,) + (1,) * (len(extent) - 1 - position))
    return gain


def bell_draw(own_key, extent, scale, reach, pieces=(), held_as=jnp.bfloat16):
    values = scale * jax.random.normal(own_key, extent, jnp.float32)
    if pieces:
        values = values * levels(own_key, extent, pieces, -0.22, 0.18)
    return jnp.clip(values, -reach, reach).astype(held_as)


def setup_inputs(seed: int = 0, part: int = 0) -> dict:
    keys = jax.random.split(jax.random.key(seed), 5)
    part_splits = jax.random.split(jax.random.fold_in(keys[4], part), 5)
    return {
        "samples": bell_draw(part_splits[0], (QUART * AGROUPS, FQ, IN_DEV, FRAME), 1.0, 6.0, ((0, 16),)),
        "fir": bell_draw(keys[1], (TAPS, FRAME), TAPS ** -0.5, 1.5, (), jnp.float32),
        "chan_assign": draw_chan_assign(jax.random.fold_in(keys[4], 71), part),
        "input_order": jax.random.permutation(keys[3], INPUTS).astype(jnp.int32),
    }


def make_table(chan_assign, frame_len):
    samples_index = jnp.arange(frame_len, dtype=jnp.int32)
    phase_index = chan_assign.astype(jnp.int32)[:, None] * samples_index[None, :] % frame_len
    angles = phase_index.astype(jnp.float32) * (2.0 * math.pi / frame_len)
    norm_scale = 1.0 / math.sqrt(frame_len)
    return jnp.stack([jnp.cos(angles) * norm_scale, -jnp.sin(angles) * norm_scale]).astype(jnp.bfloat16)

def reference(samples, fir, chan_assign, input_order):
    blocks = samples.reshape(QUART, AGROUPS, FQ, IN_DEV, FRAME)
    series = jnp.transpose(blocks, (0, 2, 1, 3, 4)).reshape(SPECTRA, INPUTS, FRAME)
    need = TAPS - 1
    padded = jnp.concatenate([jnp.zeros((need, INPUTS, FRAME), series.dtype), series], axis=0)
    accum = jnp.zeros((SPECTRA, INPUTS, FRAME), jnp.float32)
    for tap_index in range(TAPS):
        shifted = padded[need - tap_index:need - tap_index + SPECTRA].astype(jnp.float32)
        accum = accum + fir[tap_index][None, None, :] * shifted
    filtered = accum.astype(jnp.bfloat16)
    dft_table = make_table(chan_assign, FRAME).reshape(2 * NCH, FRAME)
    spectra = jnp.dot(filtered.reshape(SPECTRA * INPUTS, FRAME), dft_table.T, preferred_element_type=jnp.float32)
    spectra = spectra.astype(jnp.bfloat16).reshape(SPECTRA, INPUTS, 2, NCH)
    slot_of = jnp.argsort(input_order).astype(jnp.int32)
    spectra = jnp.take(spectra, slot_of, axis=1)
    per_chan = jnp.transpose(spectra, (3, 2, 0, 1))

    def correlate_one(chan_block):
        stacked = chan_block.reshape(2 * SPECTRA, INPUTS)
        auto_sum = jnp.dot(stacked.T, stacked, preferred_element_type=jnp.float32)
        cross_sum = jnp.dot(chan_block[0].T, chan_block[1], preferred_element_type=jnp.float32)
        row_index = lax.broadcasted_iota(jnp.int32, (INPUTS, INPUTS), 0)
        col_index = lax.broadcasted_iota(jnp.int32, (INPUTS, INPUTS), 1)
        packed = jnp.where(row_index <= col_index, auto_sum, cross_sum - cross_sum.T) / SPECTRA
        return packed.astype(jnp.bfloat16)
    return lax.map(correlate_one, per_chan)
```

```python
import math

import jax
import jax.numpy as jnp
from jax import lax
from jax.experimental import pallas as pl
from jax.experimental.pallas import tpu as pltpu
from jax.sharding import PartitionSpec as P

QUART = 4
VMEM = 60 * 1024 * 1024


def shifted(value, axis, steps):
    count = lax.axis_size(axis)
    initial, last = (max(0, -steps), min(count, count - steps))
    return lax.ppermute(value, axis, [(source, source + steps) for source in range(initial, last)])


def make_table(chan_assign, frame_len):
    samples_index = jnp.arange(frame_len, dtype=jnp.int32)
    phase_index = chan_assign[:, None] * samples_index[None, :] % frame_len
    angles = phase_index.astype(jnp.float32) * (2.0 * math.pi / frame_len)
    norm_scale = 1.0 / math.sqrt(frame_len)
    return jnp.stack([jnp.cos(angles) * norm_scale, -jnp.sin(angles) * norm_scale]).astype(
        jnp.bfloat16
    )


def spectra_kernel(x_ref, fir_ref, dft_ref, out_ref, filt):
    frames, slots, frame_len = x_ref.shape
    taps = fir_ref.shape[0]
    dests, outs, _, chan_dev, _ = out_ref.shape
    slot_tiles = slots // 16

    @pl.loop(0, slot_tiles * (frame_len // 128))
    def _(step):
        rows = pl.ds(pl.multiple_of(lax.rem(step, slot_tiles) * 16, 16), 16)
        cols = pl.ds(pl.multiple_of(lax.div(step, slot_tiles) * 128, 128), 128)
        x = [x_ref[f, rows, cols].astype(jnp.float32) for f in range(frames)]
        fir = [fir_ref[t : t + 1, cols] for t in range(taps)]
        for o in range(outs):
            accum = None
            for t in range(taps):
                if 0 <= o - t < frames:
                    term = fir[t] * x[o - t]
                    accum = term if accum is None else accum + term
            filt[o, rows, cols] = accum.astype(jnp.bfloat16)

    @pl.loop(0, outs)
    def _(o):
        result = lax.dot_general(
            dft_ref[...],
            filt[o],
            (((1,), (1,)), ((), ())),
            preferred_element_type=jnp.float32,
        ).astype(jnp.bfloat16)
        for p in range(2):
            for d in range(dests):
                begin = (p * dests + d) * chan_dev
                out_ref[d, o, p] = result[begin : begin + chan_dev]


def form_spectra(own_frames, fir, dft_table, dests):
    frames, slots, frame_len = own_frames.shape
    outs = frames + fir.shape[0] - 1
    chan_dev = dft_table.shape[1] // dests
    return pl.pallas_call(
        spectra_kernel,
        out_shape=jax.ShapeDtypeStruct((dests, outs, 2, chan_dev, slots), jnp.bfloat16),
        in_specs=[pl.BlockSpec(memory_space=pltpu.VMEM)] * 3,
        out_specs=pl.BlockSpec(memory_space=pltpu.VMEM),
        scratch_shapes=[pltpu.VMEM((outs, slots, frame_len), jnp.bfloat16)],
        compiler_params=pltpu.CompilerParams(vmem_limit_bytes=VMEM),
        name="form_spectra",
    )(own_frames, fir, dft_table.reshape(-1, frame_len))


def correlate_kernel(spec_ref, order_ref, out_ref, gathered, select, ordered):
    sources, outs, _, chan_dev, slots = spec_ref.shape
    groups = sources // QUART
    inputs = order_ref.shape[0]
    rows_total = gathered.shape[0] // chan_dev
    frames = rows_total // (2 * QUART)
    lead = outs - frames
    spectra_total = QUART * frames

    @pl.when(pl.program_id(0) == 0)
    def _():
        for p in range(2):
            for q in range(QUART):
                base = (p * QUART + q) * frames * chan_dev
                for g in range(groups):
                    cols = slice(g * slots, (g + 1) * slots)
                    source = q * groups + g
                    for f in range(frames):
                        value = spec_ref[source, f, p]
                        if q > 0 and f < lead:
                            value = (
                                value.astype(jnp.float32)
                                + spec_ref[source - groups, frames + f, p].astype(jnp.float32)
                            ).astype(jnp.bfloat16)
                        gathered[base + f * chan_dev : base + (f + 1) * chan_dev, cols] = value
        for begin in range(0, inputs, 128):
            names = lax.broadcasted_iota(jnp.int32, (128, inputs), 1)
            hit = names == order_ref[begin : begin + 128, :]
            select[begin : begin + 128, :] = hit.astype(jnp.float32).astype(jnp.bfloat16)

        @pl.loop(0, gathered.shape[0] // 256)
        def _(step):
            rows = pl.ds(pl.multiple_of(step * 256, 256), 256)
            result = jnp.dot(gathered[rows, :], select[...], preferred_element_type=jnp.float32)
            for k in range(inputs // 128):
                ordered[k, rows, :] = result[:, k * 128 : (k + 1) * 128]

    own_rows = pl.ds(pl.program_id(0), rows_total, stride=chan_dev)
    both = jnp.concatenate([ordered[k, own_rows, :] for k in range(inputs // 128)], axis=1)
    half = rows_total // 2
    turned = both.T.astype(jnp.bfloat16)
    auto_side = both.astype(jnp.bfloat16)
    cross_side = jnp.concatenate([both[half:], -both[:half]], axis=0).astype(jnp.bfloat16)
    tile = 256
    scale = 1.0 / spectra_total
    upper = lax.broadcasted_iota(jnp.int32, (tile, tile), 0) <= lax.broadcasted_iota(
        jnp.int32, (tile, tile), 1
    )
    for begin in range(0, inputs, tile):
        left = turned[begin : begin + tile]
        for other in range(0, inputs, tile):
            cols = slice(other, other + tile)
            value = None
            if other >= begin:
                value = jnp.dot(left, auto_side[:, cols], preferred_element_type=jnp.float32)
            if other <= begin:
                cross = jnp.dot(left, cross_side[:, cols], preferred_element_type=jnp.float32)
                value = cross if value is None else jnp.where(upper, value, cross)
            out_ref[0, begin : begin + tile, cols] = (value * scale).astype(jnp.bfloat16)


def correlate(received, input_order, frames):
    sources, outs, _, chan_dev, slots = received.shape
    inputs = input_order.shape[0]
    rows = 2 * QUART * frames * chan_dev
    return pl.pallas_call(
        correlate_kernel,
        grid=(chan_dev,),
        out_shape=jax.ShapeDtypeStruct((chan_dev, inputs, inputs), jnp.bfloat16),
        in_specs=[pl.BlockSpec(memory_space=pltpu.VMEM)] * 2,
        out_specs=pl.BlockSpec((1, inputs, inputs), lambda c: (c, 0, 0)),
        scratch_shapes=[
            pltpu.VMEM((rows, inputs), jnp.bfloat16),
            pltpu.VMEM((inputs, inputs), jnp.bfloat16),
            pltpu.VMEM((inputs // 128, rows, 128), jnp.float32),
        ],
        compiler_params=pltpu.CompilerParams(vmem_limit_bytes=VMEM),
        name="correlate",
    )(received, input_order[:, None])


def by_kernels(samples, fir, chan_assign, input_order):
    own_frames = samples[0]
    frames, _, frame_len = own_frames.shape
    chan_count = lax.axis_size("chan")
    dft_table = make_table(chan_assign, frame_len)
    spectra = form_spectra(own_frames, fir, dft_table, chan_count)
    received = lax.all_to_all(spectra, "chan", split_axis=0, concat_axis=0, tiled=True)
    return correlate(received, input_order, frames)


def plain(samples, fir, chan_assign, input_order):
    own_frames = samples[0]
    frames_quarter, slots_dev, frame_len = own_frames.shape
    taps_count = fir.shape[0]
    chan_count = lax.axis_size("chan")
    group_count = chan_count // QUART
    history_len = taps_count - 1
    lead_len = min(frames_quarter, history_len)
    tail_frames = own_frames[frames_quarter - lead_len :]
    pieces = shifted(tail_frames, "chan", 1 * group_count)
    extended = jnp.concatenate([pieces, own_frames], axis=0)
    dft_table = make_table(chan_assign, frame_len)
    chan_dev = chan_assign.shape[0] // chan_count
    inputs_all = input_order.shape[0]
    spectra_total = QUART * frames_quarter
    accum = jnp.zeros((frames_quarter, slots_dev, frame_len), jnp.float32)
    for tap_index in range(taps_count):
        begin = 0 + history_len - tap_index
        accum = accum + fir[tap_index][None, None, :] * extended[
            begin : begin + frames_quarter
        ].astype(jnp.float32)
    filtered = accum.astype(jnp.bfloat16)
    spectra = jnp.einsum("pcn,fin->cfpi", dft_table, filtered, preferred_element_type=jnp.float32)
    spectra = spectra.astype(jnp.bfloat16).reshape(
        chan_count, chan_dev, frames_quarter, 2, slots_dev
    )
    received = lax.all_to_all(spectra, "chan", split_axis=0, concat_axis=4, tiled=True)
    items = received.shape[1]
    row_count = received.shape[2]
    split_parts = received.reshape(items * row_count * 2 * QUART, inputs_all)
    select = (input_order[:, None] == jnp.arange(inputs_all, dtype=jnp.int32)[None, :]).astype(
        jnp.bfloat16
    )
    ordered = jnp.dot(split_parts, select, preferred_element_type=jnp.float32).astype(jnp.bfloat16)
    ordered = ordered.reshape(items, row_count, 2, QUART, inputs_all)
    stacked = ordered.reshape(items, row_count * 2 * QUART, inputs_all)
    real_rows = ordered[:, :, 0].reshape(items, row_count * QUART, inputs_all)
    imag_rows = ordered[:, :, 1].reshape(items, row_count * QUART, inputs_all)
    auto_sum = jnp.einsum("kra,krb->kab", stacked, stacked, preferred_element_type=jnp.float32)
    cross_sum = jnp.einsum("kra,krb->kab", real_rows, imag_rows, preferred_element_type=jnp.float32)
    row_index = lax.broadcasted_iota(jnp.int32, (inputs_all, inputs_all), 0)
    col_index = lax.broadcasted_iota(jnp.int32, (inputs_all, inputs_all), 1)
    upper_mask = (row_index <= col_index)[None, :, :]
    packed = (
        jnp.where(upper_mask, auto_sum, cross_sum - jnp.swapaxes(cross_sum, 1, 2)) / spectra_total
    )
    return packed.astype(jnp.bfloat16)


def on_device(samples, fir, chan_assign, input_order):
    _, frames, slots, frame_len = samples.shape
    chan_dev = chan_assign.shape[0] // lax.axis_size("chan")
    whole = slots % 256 == 0 and chan_dev % 16 == 0 and frame_len % 128 == 0
    whole = whole and fir.shape[0] - 1 <= frames and input_order.shape[0] % 256 == 0
    form = by_kernels if whole else plain
    return form(samples, fir, chan_assign, input_order)


def solution(mesh):
    in_specs = (P(("grp", "chan"), None, None, None), P(), P(), P())
    out_specs = P(("grp", "chan"), None, None)
    return jax.shard_map(
        on_device, mesh=mesh, in_specs=in_specs, out_specs=out_specs, check_vma=False
    )
```

```python
import math

import jax
import jax.numpy as jnp
from jax import lax
from jax.experimental import pallas as pl
from jax.experimental.pallas import tpu as pltpu
from jax.sharding import PartitionSpec as P

QUART = 4
VMEM = 60 * 1024 * 1024


def shifted(value, axis, steps):
    count = lax.axis_size(axis)
    initial, last = (max(0, -steps), min(count, count - steps))
    return lax.ppermute(value, axis, [(source, source + steps) for source in range(initial, last)])


def make_table(chan_assign, frame_len):
    samples_index = jnp.arange(frame_len, dtype=jnp.int32)
    phase_index = chan_assign[:, None] * samples_index[None, :] % frame_len
    angles = phase_index.astype(jnp.float32) * (2.0 * math.pi / frame_len)
    norm_scale = 1.0 / math.sqrt(frame_len)
    return jnp.stack([jnp.cos(angles) * norm_scale, -jnp.sin(angles) * norm_scale]).astype(
        jnp.bfloat16
    )


def spectra_kernel(x_ref, fir_ref, dft_ref, out_ref, filt):
    frames, slots, frame_len = x_ref.shape
    taps = fir_ref.shape[0]
    dests, outs, _, chan_dev, _ = out_ref.shape
    slot_tiles = slots // 16

    @pl.loop(0, slot_tiles * (frame_len // 128))
    def _(step):
        rows = pl.ds(pl.multiple_of(lax.rem(step, slot_tiles) * 16, 16), 16)
        cols = pl.ds(pl.multiple_of(lax.div(step, slot_tiles) * 128, 128), 128)
        x = [x_ref[f, rows, cols].astype(jnp.float32) for f in range(frames)]
        fir = [fir_ref[t : t + 1, cols] for t in range(taps)]
        for o in range(outs):
            accum = None
            for t in range(taps):
                if 0 <= o - t < frames:
                    term = fir[t] * x[o - t]
                    accum = term if accum is None else accum + term
            filt[o, rows, cols] = accum.astype(jnp.bfloat16)

    @pl.loop(0, outs)
    def _(o):
        result = lax.dot_general(
            dft_ref[...],
            filt[o],
            (((1,), (1,)), ((), ())),
            preferred_element_type=jnp.float32,
        ).astype(jnp.bfloat16)
        for p in range(2):
            for d in range(dests):
                begin = (p * dests + d) * chan_dev
                out_ref[d, o, p] = result[begin : begin + chan_dev]


def form_spectra(own_frames, fir, dft_table, dests):
    frames, slots, frame_len = own_frames.shape
    outs = frames + fir.shape[0] - 1
    chan_dev = dft_table.shape[1] // dests
    return pl.pallas_call(
        spectra_kernel,
        out_shape=jax.ShapeDtypeStruct((dests, outs, 2, chan_dev, slots), jnp.bfloat16),
        in_specs=[pl.BlockSpec(memory_space=pltpu.VMEM)] * 3,
        out_specs=pl.BlockSpec(memory_space=pltpu.VMEM),
        scratch_shapes=[pltpu.VMEM((outs, slots, frame_len), jnp.bfloat16)],
        compiler_params=pltpu.CompilerParams(vmem_limit_bytes=VMEM),
        name="form_spectra",
    )(own_frames, fir, dft_table.reshape(-1, frame_len))


def exchange_kernel(
    spec_ref, recv_ref, merged, own_send, own_recv, tail_send, tail_recv, lead_send, lead_recv, local
):
    dests, outs, _, _, _ = spec_ref.shape
    frames = merged.shape[1]
    lead = outs - frames
    groups = dests // QUART
    me = lax.axis_index("chan")
    quarter = lax.div(me, groups)
    after = lax.rem(me + groups, dests)
    part = lax.axis_index("grp")
    head, tail = pl.ds(0, frames), pl.ds(frames, lead)

    def remote(src, dst, send, recv, device):
        return pltpu.make_async_remote_copy(
            src_ref=src,
            dst_ref=dst,
            send_sem=send,
            recv_sem=recv,
            device_id=(part, device),
            device_id_type=pl.DeviceIdType.MESH,
        )

    def send_own(d):
        return remote(
            spec_ref.at[d, head], recv_ref.at[me, head], own_send.at[d], own_recv.at[me], d
        )

    def send_merged(d):
        return remote(merged.at[d], recv_ref.at[me, head], own_send.at[d], own_recv.at[me], d)

    def send_tail(d):
        return remote(
            spec_ref.at[d, tail], recv_ref.at[me, tail], tail_send.at[d], tail_recv.at[me], d
        )

    def send_lead(d):
        return remote(
            spec_ref.at[d, tail],
            merged.at[d, pl.ds(0, lead)],
            lead_send.at[d],
            lead_recv.at[d],
            after,
        )

    barrier = pltpu.get_barrier_semaphore()

    @pl.loop(1, dests)
    def _(k):
        other = lax.rem(me + k, dests)
        pl.semaphore_signal(
            barrier, inc=1, device_id=(part, other), device_id_type=pl.DeviceIdType.MESH
        )

    pl.semaphore_wait(barrier, dests - 1)
    has_tail = quarter < QUART - 1
    stay = pltpu.make_async_copy(spec_ref.at[me], recv_ref.at[me], local)

    @pl.loop(0, dests)
    def _(d):
        @pl.when(quarter < lax.div(d, groups) - 1)
        def _():
            send_lead(d).start()

    @pl.loop(1, dests)
    def _(k):
        d = lax.rem(me + k, dests)

        @pl.when(quarter >= lax.div(d, groups))
        def _():
            send_own(d).start()

            @pl.when(has_tail)
            def _():
                send_tail(d).start()

    stay.start()

    @pl.loop(0, dests)
    def _(d):
        @pl.when(quarter < lax.div(d, groups) - 1)
        def _():
            send_lead(d).wait_send()

    @pl.loop(1, dests)
    def _(k):
        d = lax.rem(me + dests - k, dests)
        target = lax.div(d, groups)

        @pl.when((quarter == 0) & (target > 0))
        def _():
            send_own(d).start()

        @pl.when(quarter == target - 1)
        def _():
            send_tail(d).start()

    @pl.loop(0, dests)
    def _(d):
        @pl.when((quarter >= 1) & (quarter < lax.div(d, groups)))
        def _():
            send_lead(d).wait_recv()

            @pl.loop(0, lead)
            def _(f):
                merged[d, f] = (
                    merged[d, f].astype(jnp.float32) + spec_ref[d, f].astype(jnp.float32)
                ).astype(jnp.bfloat16)

            for f in range(lead, frames):
                merged[d, f] = spec_ref[d, f]
            send_merged(d).start()

    stay.wait()

    @pl.loop(1, dests)
    def _(k):
        d = lax.rem(me + k, dests)
        target = lax.div(d, groups)
        send_own(d).wait_send()

        @pl.when(has_tail & (quarter >= target - 1))
        def _():
            send_tail(d).wait_send()

        remote(
            spec_ref.at[d, head], recv_ref.at[d, head], own_send.at[d], own_recv.at[d], d
        ).wait_recv()

        @pl.when((target < QUART - 1) & (target >= quarter - 1))
        def _():
            remote(
                spec_ref.at[d, tail], recv_ref.at[d, tail], tail_send.at[d], tail_recv.at[d], d
            ).wait_recv()


def exchange(spectra, frames):
    dests, outs, two, chan_dev, slots = spectra.shape
    copies = pltpu.SemaphoreType.DMA((dests,))
    return pl.pallas_call(
        exchange_kernel,
        out_shape=jax.ShapeDtypeStruct(spectra.shape, spectra.dtype),
        in_specs=[pl.BlockSpec(memory_space=pltpu.VMEM)],
        out_specs=pl.BlockSpec(memory_space=pl.ANY),
        scratch_shapes=[pltpu.VMEM((dests, frames, two, chan_dev, slots), spectra.dtype)]
        + [copies] * 6
        + [pltpu.SemaphoreType.DMA],
        compiler_params=pltpu.CompilerParams(
            collective_id=0, has_side_effects=True, vmem_limit_bytes=VMEM
        ),
        name="exchange",
    )(spectra)


def correlate_kernel(spec_ref, order_ref, out_ref, gathered, select, ordered):
    sources, outs, _, chan_dev, slots = spec_ref.shape
    groups = sources // QUART
    inputs = order_ref.shape[0]
    rows_total = gathered.shape[0] // chan_dev
    frames = rows_total // (2 * QUART)
    lead = outs - frames
    spectra_total = QUART * frames

    quarter = lax.div(lax.axis_index("chan"), groups)

    def gather(q, add):
        for p in range(2):
            base = (p * QUART + q) * frames * chan_dev
            for g in range(groups):
                cols = slice(g * slots, (g + 1) * slots)
                source = q * groups + g
                for f in range(frames):
                    value = spec_ref[source, f, p]
                    if add and f < lead:
                        value = (
                            value.astype(jnp.float32)
                            + spec_ref[source - groups, frames + f, p].astype(jnp.float32)
                        ).astype(jnp.bfloat16)
                    gathered[base + f * chan_dev : base + (f + 1) * chan_dev, cols] = value

    @pl.when(pl.program_id(0) == 0)
    def _():
        gather(0, False)
        for q in range(1, QUART):
            pl.when(q >= quarter)(lambda q=q: gather(q, True))
            pl.when(q < quarter)(lambda q=q: gather(q, False))
        for begin in range(0, inputs, 128):
            names = lax.broadcasted_iota(jnp.int32, (128, inputs), 1)
            hit = names == order_ref[begin : begin + 128, :]
            select[begin : begin + 128, :] = hit.astype(jnp.float32).astype(jnp.bfloat16)

        @pl.loop(0, gathered.shape[0] // 256)
        def _(step):
            rows = pl.ds(pl.multiple_of(step * 256, 256), 256)
            result = jnp.dot(gathered[rows, :], select[...], preferred_element_type=jnp.float32)
            for k in range(inputs // 128):
                ordered[k, rows, :] = result[:, k * 128 : (k + 1) * 128]

    own_rows = pl.ds(pl.program_id(0), rows_total, stride=chan_dev)
    both = jnp.concatenate([ordered[k, own_rows, :] for k in range(inputs // 128)], axis=1)
    half = rows_total // 2
    turned = both.T.astype(jnp.bfloat16)
    auto_side = both.astype(jnp.bfloat16)
    cross_side = jnp.concatenate([both[half:], -both[:half]], axis=0).astype(jnp.bfloat16)
    tile = 256
    scale = 1.0 / spectra_total
    upper = lax.broadcasted_iota(jnp.int32, (tile, tile), 0) <= lax.broadcasted_iota(
        jnp.int32, (tile, tile), 1
    )
    for begin in range(0, inputs, tile):
        left = turned[begin : begin + tile]
        for other in range(0, inputs, tile):
            cols = slice(other, other + tile)
            value = None
            if other >= begin:
                value = jnp.dot(left, auto_side[:, cols], preferred_element_type=jnp.float32)
            if other <= begin:
                cross = jnp.dot(left, cross_side[:, cols], preferred_element_type=jnp.float32)
                value = cross if value is None else jnp.where(upper, value, cross)
            out_ref[0, begin : begin + tile, cols] = (value * scale).astype(jnp.bfloat16)


def correlate(received, input_order, frames):
    sources, outs, _, chan_dev, slots = received.shape
    inputs = input_order.shape[0]
    rows = 2 * QUART * frames * chan_dev
    return pl.pallas_call(
        correlate_kernel,
        grid=(chan_dev,),
        out_shape=jax.ShapeDtypeStruct((chan_dev, inputs, inputs), jnp.bfloat16),
        in_specs=[pl.BlockSpec(memory_space=pltpu.VMEM)] * 2,
        out_specs=pl.BlockSpec((1, inputs, inputs), lambda c: (c, 0, 0)),
        scratch_shapes=[
            pltpu.VMEM((rows, inputs), jnp.bfloat16),
            pltpu.VMEM((inputs, inputs), jnp.bfloat16),
            pltpu.VMEM((inputs // 128, rows, 128), jnp.float32),
        ],
        compiler_params=pltpu.CompilerParams(vmem_limit_bytes=VMEM),
        name="correlate",
    )(received, input_order[:, None])


def by_kernels(samples, fir, chan_assign, input_order):
    own_frames = samples[0]
    frames, _, frame_len = own_frames.shape
    chan_count = lax.axis_size("chan")
    dft_table = make_table(chan_assign, frame_len)
    spectra = form_spectra(own_frames, fir, dft_table, chan_count)
    received = exchange(spectra, frames)
    return correlate(received, input_order, frames)


def plain(samples, fir, chan_assign, input_order):
    own_frames = samples[0]
    frames_quarter, slots_dev, frame_len = own_frames.shape
    taps_count = fir.shape[0]
    chan_count = lax.axis_size("chan")
    group_count = chan_count // QUART
    history_len = taps_count - 1
    lead_len = min(frames_quarter, history_len)
    tail_frames = own_frames[frames_quarter - lead_len :]
    pieces = shifted(tail_frames, "chan", 1 * group_count)
    extended = jnp.concatenate([pieces, own_frames], axis=0)
    dft_table = make_table(chan_assign, frame_len)
    chan_dev = chan_assign.shape[0] // chan_count
    inputs_all = input_order.shape[0]
    spectra_total = QUART * frames_quarter
    accum = jnp.zeros((frames_quarter, slots_dev, frame_len), jnp.float32)
    for tap_index in range(taps_count):
        begin = 0 + history_len - tap_index
        accum = accum + fir[tap_index][None, None, :] * extended[
            begin : begin + frames_quarter
        ].astype(jnp.float32)
    filtered = accum.astype(jnp.bfloat16)
    spectra = jnp.einsum("pcn,fin->cfpi", dft_table, filtered, preferred_element_type=jnp.float32)
    spectra = spectra.astype(jnp.bfloat16).reshape(
        chan_count, chan_dev, frames_quarter, 2, slots_dev
    )
    received = lax.all_to_all(spectra, "chan", split_axis=0, concat_axis=4, tiled=True)
    items = received.shape[1]
    row_count = received.shape[2]
    split_parts = received.reshape(items * row_count * 2 * QUART, inputs_all)
    select = (input_order[:, None] == jnp.arange(inputs_all, dtype=jnp.int32)[None, :]).astype(
        jnp.bfloat16
    )
    ordered = jnp.dot(split_parts, select, preferred_element_type=jnp.float32).astype(jnp.bfloat16)
    ordered = ordered.reshape(items, row_count, 2, QUART, inputs_all)
    stacked = ordered.reshape(items, row_count * 2 * QUART, inputs_all)
    real_rows = ordered[:, :, 0].reshape(items, row_count * QUART, inputs_all)
    imag_rows = ordered[:, :, 1].reshape(items, row_count * QUART, inputs_all)
    auto_sum = jnp.einsum("kra,krb->kab", stacked, stacked, preferred_element_type=jnp.float32)
    cross_sum = jnp.einsum("kra,krb->kab", real_rows, imag_rows, preferred_element_type=jnp.float32)
    row_index = lax.broadcasted_iota(jnp.int32, (inputs_all, inputs_all), 0)
    col_index = lax.broadcasted_iota(jnp.int32, (inputs_all, inputs_all), 1)
    upper_mask = (row_index <= col_index)[None, :, :]
    packed = (
        jnp.where(upper_mask, auto_sum, cross_sum - jnp.swapaxes(cross_sum, 1, 2)) / spectra_total
    )
    return packed.astype(jnp.bfloat16)


def on_device(samples, fir, chan_assign, input_order):
    _, frames, slots, frame_len = samples.shape
    chan_dev = chan_assign.shape[0] // lax.axis_size("chan")
    whole = slots % 256 == 0 and chan_dev % 16 == 0 and frame_len % 128 == 0
    whole = whole and fir.shape[0] - 1 <= frames and input_order.shape[0] % 256 == 0
    form = by_kernels if whole else plain
    return form(samples, fir, chan_assign, input_order)


def solution(mesh):
    in_specs = (P(("grp", "chan"), None, None, None), P(), P(), P())
    out_specs = P(("grp", "chan"), None, None)
    return jax.shard_map(
        on_device, mesh=mesh, in_specs=in_specs, out_specs=out_specs, check_vma=False
    )
```

```python
import math

import jax
import jax.numpy as jnp
from jax import lax
from jax.experimental import pallas as pl
from jax.experimental.pallas import tpu as pltpu
from jax.sharding import PartitionSpec as P

QUART = 4
VMEM = 60 * 1024 * 1024


def shifted(value, axis, steps):
    count = lax.axis_size(axis)
    initial, last = (max(0, -steps), min(count, count - steps))
    return lax.ppermute(value, axis, [(source, source + steps) for source in range(initial, last)])


def make_table(chan_assign, frame_len):
    samples_index = jnp.arange(frame_len, dtype=jnp.int32)
    phase_index = chan_assign[:, None] * samples_index[None, :] % frame_len
    angles = phase_index.astype(jnp.float32) * (2.0 * math.pi / frame_len)
    norm_scale = 1.0 / math.sqrt(frame_len)
    return jnp.stack([jnp.cos(angles) * norm_scale, -jnp.sin(angles) * norm_scale]).astype(
        jnp.bfloat16
    )


def phase_parts(chan_assign, frame_len):
    def turn(steps):
        phase = chan_assign[:, None] * steps[None, :] % frame_len
        angles = phase.astype(jnp.float32) * (2.0 * math.pi / frame_len)
        return jnp.stack([jnp.cos(angles), jnp.sin(angles)])

    high = turn(128 * jnp.arange(frame_len // 128, dtype=jnp.int32))
    return high, turn(jnp.arange(128, dtype=jnp.int32))


def fill_table(high_ref, low_ref, table):
    chans = low_ref.shape[1]
    frame_len = table.shape[1]
    scale = 1.0 / math.sqrt(frame_len)
    cos_low, sin_low = low_ref[0], low_ref[1]
    for h in range(frame_len // 128):
        cos_high, sin_high = high_ref[0, :, h : h + 1], high_ref[1, :, h : h + 1]
        cols = slice(h * 128, (h + 1) * 128)
        real = (cos_high * cos_low - sin_high * sin_low) * scale
        imag = (sin_high * cos_low + cos_high * sin_low) * -scale
        table[:chans, cols] = real.astype(jnp.bfloat16)
        table[chans:, cols] = imag.astype(jnp.bfloat16)


def form(x_ref, fir_ref, table, filt, spec_ref, first, count):
    frames, slots, frame_len = x_ref.shape
    taps = fir_ref.shape[0]
    dests, _, _, chan_dev, _ = spec_ref.shape
    slot_tiles = slots // 16

    @pl.loop(0, slot_tiles * (frame_len // 128))
    def _(step):
        rows = pl.ds(pl.multiple_of(lax.rem(step, slot_tiles) * 16, 16), 16)
        cols = pl.ds(pl.multiple_of(lax.div(step, slot_tiles) * 128, 128), 128)
        x = [x_ref[f, rows, cols].astype(jnp.float32) for f in range(frames)]
        fir = [fir_ref[t : t + 1, cols] for t in range(taps)]
        for o in range(first, first + count):
            accum = None
            for t in range(taps):
                if 0 <= o - t < frames:
                    term = fir[t] * x[o - t]
                    accum = term if accum is None else accum + term
            filt[o - first, rows, cols] = accum.astype(jnp.bfloat16)

    @pl.loop(0, count)
    def _(o):
        result = lax.dot_general(
            table[...],
            filt[o],
            (((1,), (1,)), ((), ())),
            preferred_element_type=jnp.float32,
        ).astype(jnp.bfloat16)
        for p in range(2):
            for d in range(dests):
                begin = (p * dests + d) * chan_dev
                spec_ref[d, first + o, p] = result[begin : begin + chan_dev]


def exchange_kernel(
    x_ref,
    fir_ref,
    high_ref,
    low_ref,
    recv_ref,
    table,
    filt,
    spec_ref,
    merged,
    own_send,
    own_recv,
    tail_send,
    tail_recv,
    lead_send,
    lead_recv,
    local,
):
    dests, outs, _, _, _ = spec_ref.shape
    frames = merged.shape[1]
    lead = outs - frames
    groups = dests // QUART
    me = lax.axis_index("chan")
    quarter = lax.div(me, groups)
    after = lax.rem(me + groups, dests)
    part = lax.axis_index("grp")
    head, tail = pl.ds(0, frames), pl.ds(frames, lead)

    def remote(src, dst, send, recv, device):
        return pltpu.make_async_remote_copy(
            src_ref=src,
            dst_ref=dst,
            send_sem=send,
            recv_sem=recv,
            device_id=(part, device),
            device_id_type=pl.DeviceIdType.MESH,
        )

    def send_own(d):
        return remote(
            spec_ref.at[d, head], recv_ref.at[me, head], own_send.at[d], own_recv.at[me], d
        )

    def send_merged(d):
        return remote(merged.at[d], recv_ref.at[me, head], own_send.at[d], own_recv.at[me], d)

    def send_tail(d):
        return remote(
            spec_ref.at[d, tail], recv_ref.at[me, tail], tail_send.at[d], tail_recv.at[me], d
        )

    def send_lead(d):
        return remote(
            spec_ref.at[d, tail],
            merged.at[d, pl.ds(0, lead)],
            lead_send.at[d],
            lead_recv.at[d],
            after,
        )

    barrier = pltpu.get_barrier_semaphore()

    @pl.loop(1, dests)
    def _(k):
        other = lax.rem(me + k, dests)
        pl.semaphore_signal(
            barrier, inc=1, device_id=(part, other), device_id_type=pl.DeviceIdType.MESH
        )

    pl.semaphore_wait(barrier, dests - 1)
    has_tail = quarter < QUART - 1
    no_lead = quarter >= QUART - 2
    stay = pltpu.make_async_copy(spec_ref.at[me, head], recv_ref.at[me, head], local.at[0])
    stay_tail = pltpu.make_async_copy(spec_ref.at[me, tail], recv_ref.at[me, tail], local.at[1])
    fill_table(high_ref, low_ref, table)

    @pl.when(has_tail)
    def _():
        form(x_ref, fir_ref, table, filt, spec_ref, frames, lead)
        stay_tail.start()

        @pl.loop(0, dests)
        def _(d):
            @pl.when(quarter < lax.div(d, groups) - 1)
            def _():
                send_lead(d).start()

        @pl.loop(1, dests)
        def _(k):
            d = lax.rem(me + k, dests)

            @pl.when(no_lead | (quarter >= lax.div(d, groups)))
            def _():
                send_tail(d).start()

    form(x_ref, fir_ref, table, filt, spec_ref, 0, frames)

    @pl.loop(1, dests)
    def _(k):
        d = lax.rem(me + k, dests)

        @pl.when(quarter >= lax.div(d, groups))
        def _():
            send_own(d).start()

    stay.start()

    @pl.loop(0, dests)
    def _(d):
        @pl.when(quarter < lax.div(d, groups) - 1)
        def _():
            send_lead(d).wait_send()

    @pl.loop(1, dests)
    def _(k):
        d = lax.rem(me + dests - k, dests)
        target = lax.div(d, groups)

        @pl.when((quarter == 0) & (target > 0))
        def _():
            send_own(d).start()

        @pl.when((quarter < QUART - 2) & (quarter == target - 1))
        def _():
            send_tail(d).start()

    @pl.loop(0, dests)
    def _(d):
        @pl.when((quarter >= 1) & (quarter < lax.div(d, groups)))
        def _():
            send_lead(d).wait_recv()

            @pl.loop(0, lead)
            def _(f):
                merged[d, f] = (
                    merged[d, f].astype(jnp.float32) + spec_ref[d, f].astype(jnp.float32)
                ).astype(jnp.bfloat16)

            for f in range(lead, frames):
                merged[d, f] = spec_ref[d, f]
            send_merged(d).start()

    stay.wait()
    pl.when(has_tail)(stay_tail.wait)

    @pl.loop(1, dests)
    def _(k):
        d = lax.rem(me + k, dests)
        target = lax.div(d, groups)
        send_own(d).wait_send()

        @pl.when(has_tail & (quarter >= target - 1))
        def _():
            send_tail(d).wait_send()

        remote(
            spec_ref.at[d, head], recv_ref.at[d, head], own_send.at[d], own_recv.at[d], d
        ).wait_recv()

        @pl.when((target < QUART - 1) & (target >= quarter - 1))
        def _():
            remote(
                spec_ref.at[d, tail], recv_ref.at[d, tail], tail_send.at[d], tail_recv.at[d], d
            ).wait_recv()


def exchange(own_frames, fir, high, low, dests):
    frames, slots, frame_len = own_frames.shape
    lead = fir.shape[0] - 1
    chans = low.shape[1]
    chan_dev = chans // dests
    spectra = (dests, frames + lead, 2, chan_dev, slots)
    copies = pltpu.SemaphoreType.DMA((dests,))
    return pl.pallas_call(
        exchange_kernel,
        out_shape=jax.ShapeDtypeStruct(spectra, jnp.bfloat16),
        in_specs=[pl.BlockSpec(memory_space=pltpu.VMEM)] * 4,
        out_specs=pl.BlockSpec(memory_space=pl.ANY),
        scratch_shapes=[
            pltpu.VMEM((2 * chans, frame_len), jnp.bfloat16),
            pltpu.VMEM((frames, slots, frame_len), jnp.bfloat16),
            pltpu.VMEM(spectra, jnp.bfloat16),
            pltpu.VMEM((dests, frames, 2, chan_dev, slots), jnp.bfloat16),
        ]
        + [copies] * 6
        + [pltpu.SemaphoreType.DMA((2,))],
        compiler_params=pltpu.CompilerParams(
            collective_id=0, has_side_effects=True, vmem_limit_bytes=VMEM
        ),
        name="exchange",
    )(own_frames, fir, high, low)


def correlate_kernel(spec_ref, order_ref, out_ref, gathered, select, ordered):
    sources, outs, _, chan_dev, slots = spec_ref.shape
    groups = sources // QUART
    inputs = order_ref.shape[0]
    rows_total = gathered.shape[0] // chan_dev
    frames = rows_total // (2 * QUART)
    lead = outs - frames
    spectra_total = QUART * frames

    quarter = lax.div(lax.axis_index("chan"), groups)

    def gather(q, add):
        for p in range(2):
            base = (p * QUART + q) * frames * chan_dev
            for g in range(groups):
                cols = slice(g * slots, (g + 1) * slots)
                source = q * groups + g
                for f in range(frames):
                    value = spec_ref[source, f, p]
                    if add and f < lead:
                        value = (
                            value.astype(jnp.float32)
                            + spec_ref[source - groups, frames + f, p].astype(jnp.float32)
                        ).astype(jnp.bfloat16)
                    gathered[base + f * chan_dev : base + (f + 1) * chan_dev, cols] = value

    @pl.when(pl.program_id(0) == 0)
    def _():
        gather(0, False)
        for q in range(1, QUART):
            pl.when(q >= quarter)(lambda q=q: gather(q, True))
            pl.when(q < quarter)(lambda q=q: gather(q, False))
        for begin in range(0, inputs, 128):
            names = lax.broadcasted_iota(jnp.int32, (128, inputs), 1)
            hit = names == order_ref[begin : begin + 128, :]
            select[begin : begin + 128, :] = hit.astype(jnp.float32).astype(jnp.bfloat16)

        @pl.loop(0, gathered.shape[0] // 256)
        def _(step):
            rows = pl.ds(pl.multiple_of(step * 256, 256), 256)
            result = jnp.dot(gathered[rows, :], select[...], preferred_element_type=jnp.float32)
            for k in range(inputs // 128):
                ordered[k, rows, :] = result[:, k * 128 : (k + 1) * 128]

    own_rows = pl.ds(pl.program_id(0), rows_total, stride=chan_dev)
    both = jnp.concatenate([ordered[k, own_rows, :] for k in range(inputs // 128)], axis=1)
    half = rows_total // 2
    turned = both.T.astype(jnp.bfloat16)
    auto_side = both.astype(jnp.bfloat16)
    cross_side = jnp.concatenate([both[half:], -both[:half]], axis=0).astype(jnp.bfloat16)
    tile = 256
    scale = 1.0 / spectra_total
    upper = lax.broadcasted_iota(jnp.int32, (tile, tile), 0) <= lax.broadcasted_iota(
        jnp.int32, (tile, tile), 1
    )
    for begin in range(0, inputs, tile):
        left = turned[begin : begin + tile]
        for other in range(0, inputs, tile):
            cols = slice(other, other + tile)
            value = None
            if other >= begin:
                value = jnp.dot(left, auto_side[:, cols], preferred_element_type=jnp.float32)
            if other <= begin:
                cross = jnp.dot(left, cross_side[:, cols], preferred_element_type=jnp.float32)
                value = cross if value is None else jnp.where(upper, value, cross)
            out_ref[0, begin : begin + tile, cols] = (value * scale).astype(jnp.bfloat16)


def correlate(received, input_order, frames):
    sources, outs, _, chan_dev, slots = received.shape
    inputs = input_order.shape[0]
    rows = 2 * QUART * frames * chan_dev
    return pl.pallas_call(
        correlate_kernel,
        grid=(chan_dev,),
        out_shape=jax.ShapeDtypeStruct((chan_dev, inputs, inputs), jnp.bfloat16),
        in_specs=[pl.BlockSpec(memory_space=pltpu.VMEM)] * 2,
        out_specs=pl.BlockSpec((1, inputs, inputs), lambda c: (c, 0, 0)),
        scratch_shapes=[
            pltpu.VMEM((rows, inputs), jnp.bfloat16),
            pltpu.VMEM((inputs, inputs), jnp.bfloat16),
            pltpu.VMEM((inputs // 128, rows, 128), jnp.float32),
        ],
        compiler_params=pltpu.CompilerParams(vmem_limit_bytes=VMEM),
        name="correlate",
    )(received, input_order[:, None])


def by_kernels(samples, fir, chan_assign, input_order):
    own_frames = samples[0]
    frames, _, frame_len = own_frames.shape
    chan_count = lax.axis_size("chan")
    high, low = phase_parts(chan_assign, frame_len)
    received = exchange(own_frames, fir, high, low, chan_count)
    return correlate(received, input_order, frames)


def plain(samples, fir, chan_assign, input_order):
    own_frames = samples[0]
    frames_quarter, slots_dev, frame_len = own_frames.shape
    taps_count = fir.shape[0]
    chan_count = lax.axis_size("chan")
    group_count = chan_count // QUART
    history_len = taps_count - 1
    lead_len = min(frames_quarter, history_len)
    tail_frames = own_frames[frames_quarter - lead_len :]
    pieces = shifted(tail_frames, "chan", 1 * group_count)
    extended = jnp.concatenate([pieces, own_frames], axis=0)
    dft_table = make_table(chan_assign, frame_len)
    chan_dev = chan_assign.shape[0] // chan_count
    inputs_all = input_order.shape[0]
    spectra_total = QUART * frames_quarter
    accum = jnp.zeros((frames_quarter, slots_dev, frame_len), jnp.float32)
    for tap_index in range(taps_count):
        begin = 0 + history_len - tap_index
        accum = accum + fir[tap_index][None, None, :] * extended[
            begin : begin + frames_quarter
        ].astype(jnp.float32)
    filtered = accum.astype(jnp.bfloat16)
    spectra = jnp.einsum("pcn,fin->cfpi", dft_table, filtered, preferred_element_type=jnp.float32)
    spectra = spectra.astype(jnp.bfloat16).reshape(
        chan_count, chan_dev, frames_quarter, 2, slots_dev
    )
    received = lax.all_to_all(spectra, "chan", split_axis=0, concat_axis=4, tiled=True)
    items = received.shape[1]
    row_count = received.shape[2]
    split_parts = received.reshape(items * row_count * 2 * QUART, inputs_all)
    select = (input_order[:, None] == jnp.arange(inputs_all, dtype=jnp.int32)[None, :]).astype(
        jnp.bfloat16
    )
    ordered = jnp.dot(split_parts, select, preferred_element_type=jnp.float32).astype(jnp.bfloat16)
    ordered = ordered.reshape(items, row_count, 2, QUART, inputs_all)
    stacked = ordered.reshape(items, row_count * 2 * QUART, inputs_all)
    real_rows = ordered[:, :, 0].reshape(items, row_count * QUART, inputs_all)
    imag_rows = ordered[:, :, 1].reshape(items, row_count * QUART, inputs_all)
    auto_sum = jnp.einsum("kra,krb->kab", stacked, stacked, preferred_element_type=jnp.float32)
    cross_sum = jnp.einsum("kra,krb->kab", real_rows, imag_rows, preferred_element_type=jnp.float32)
    row_index = lax.broadcasted_iota(jnp.int32, (inputs_all, inputs_all), 0)
    col_index = lax.broadcasted_iota(jnp.int32, (inputs_all, inputs_all), 1)
    upper_mask = (row_index <= col_index)[None, :, :]
    packed = (
        jnp.where(upper_mask, auto_sum, cross_sum - jnp.swapaxes(cross_sum, 1, 2)) / spectra_total
    )
    return packed.astype(jnp.bfloat16)


def on_device(samples, fir, chan_assign, input_order):
    _, frames, slots, frame_len = samples.shape
    chan_dev = chan_assign.shape[0] // lax.axis_size("chan")
    whole = slots % 256 == 0 and chan_dev % 16 == 0 and frame_len % 128 == 0
    whole = whole and fir.shape[0] - 1 <= frames and input_order.shape[0] % 256 == 0
    form = by_kernels if whole else plain
    return form(samples, fir, chan_assign, input_order)


def solution(mesh):
    in_specs = (P(("grp", "chan"), None, None, None), P(), P(), P())
    out_specs = P(("grp", "chan"), None, None)
    return jax.shard_map(
        on_device, mesh=mesh, in_specs=in_specs, out_specs=out_specs, check_vma=False
    )
```

```python
import math

import jax
import jax.numpy as jnp
from jax import lax
from jax.experimental import pallas as pl
from jax.experimental.pallas import tpu as pltpu
from jax.sharding import PartitionSpec as P

QUART = 4
VMEM = 60 * 1024 * 1024


def shifted(value, axis, steps):
    count = lax.axis_size(axis)
    initial, last = (max(0, -steps), min(count, count - steps))
    return lax.ppermute(value, axis, [(source, source + steps) for source in range(initial, last)])


def make_table(chan_assign, frame_len):
    samples_index = jnp.arange(frame_len, dtype=jnp.int32)
    phase_index = chan_assign[:, None] * samples_index[None, :] % frame_len
    angles = phase_index.astype(jnp.float32) * (2.0 * math.pi / frame_len)
    norm_scale = 1.0 / math.sqrt(frame_len)
    return jnp.stack([jnp.cos(angles) * norm_scale, -jnp.sin(angles) * norm_scale]).astype(
        jnp.bfloat16
    )


def phase_parts(chan_assign, frame_len):
    def turn(steps):
        phase = chan_assign[:, None] * steps[None, :] % frame_len
        angles = phase.astype(jnp.float32) * (2.0 * math.pi / frame_len)
        return jnp.stack([jnp.cos(angles), jnp.sin(angles)])

    high = turn(128 * jnp.arange(frame_len // 128, dtype=jnp.int32))
    return high, turn(jnp.arange(128, dtype=jnp.int32))


def fill_table(high_ref, low_ref, table):
    chans = low_ref.shape[1]
    frame_len = table.shape[1]
    scale = 1.0 / math.sqrt(frame_len)
    cos_low, sin_low = low_ref[0], low_ref[1]
    for h in range(frame_len // 128):
        cos_high, sin_high = high_ref[0, :, h : h + 1], high_ref[1, :, h : h + 1]
        cols = slice(h * 128, (h + 1) * 128)
        real = (cos_high * cos_low - sin_high * sin_low) * scale
        imag = (sin_high * cos_low + cos_high * sin_low) * -scale
        table[:chans, cols] = real.astype(jnp.bfloat16)
        table[chans:, cols] = imag.astype(jnp.bfloat16)


def form(x_ref, fir_ref, table, filt, spec_ref, first, count):
    frames, slots, frame_len = x_ref.shape
    taps = fir_ref.shape[0]
    dests, _, _, chan_dev, _ = spec_ref.shape
    slot_tiles = slots // 16

    @pl.loop(0, slot_tiles * (frame_len // 128))
    def _(step):
        rows = pl.ds(pl.multiple_of(lax.rem(step, slot_tiles) * 16, 16), 16)
        cols = pl.ds(pl.multiple_of(lax.div(step, slot_tiles) * 128, 128), 128)
        x = [x_ref[f, rows, cols].astype(jnp.float32) for f in range(frames)]
        fir = [fir_ref[t : t + 1, cols] for t in range(taps)]
        for o in range(first, first + count):
            accum = None
            for t in range(taps):
                if 0 <= o - t < frames:
                    term = fir[t] * x[o - t]
                    accum = term if accum is None else accum + term
            filt[o - first, rows, cols] = accum.astype(jnp.bfloat16)

    @pl.loop(0, count)
    def _(o):
        result = lax.dot_general(
            table[...],
            filt[o],
            (((1,), (1,)), ((), ())),
            preferred_element_type=jnp.float32,
        ).astype(jnp.bfloat16)
        for p in range(2):
            for d in range(dests):
                begin = (p * dests + d) * chan_dev
                spec_ref[d, first + o, p] = result[begin : begin + chan_dev]


def exchange_kernel(
    x_ref,
    fir_ref,
    high_ref,
    low_ref,
    recv_ref,
    table,
    filt,
    spec_ref,
    merged,
    own_send,
    own_recv,
    tail_send,
    tail_recv,
    lead_send,
    lead_recv,
    local,
):
    dests, outs, _, _, _ = spec_ref.shape
    frames = merged.shape[1]
    lead = outs - frames
    groups = dests // QUART
    me = lax.axis_index("chan")
    quarter = lax.div(me, groups)
    after = lax.rem(me + groups, dests)
    part = lax.axis_index("grp")
    head, tail = pl.ds(0, frames), pl.ds(frames, lead)
    split = (lead + 1) // 2
    parts = ((split, lead - split), (0, split))

    def remote(src, dst, send, recv, device):
        return pltpu.make_async_remote_copy(
            src_ref=src,
            dst_ref=dst,
            send_sem=send,
            recv_sem=recv,
            device_id=(part, device),
            device_id_type=pl.DeviceIdType.MESH,
        )

    def send_own(d):
        return remote(
            spec_ref.at[d, head], recv_ref.at[me, head], own_send.at[d], own_recv.at[me], d
        )

    def send_merged(d):
        return remote(merged.at[d], recv_ref.at[me, head], own_send.at[d], own_recv.at[me], d)

    def send_tail(d, h):
        here = pl.ds(frames + parts[h][0], parts[h][1])
        return remote(
            spec_ref.at[d, here],
            recv_ref.at[me, here],
            tail_send.at[h, d],
            tail_recv.at[h, me],
            d,
        )

    def send_lead(d, h):
        begin, count = parts[h]
        return remote(
            spec_ref.at[d, pl.ds(frames + begin, count)],
            merged.at[d, pl.ds(begin, count)],
            lead_send.at[h, d],
            lead_recv.at[h, d],
            after,
        )

    barrier = pltpu.get_barrier_semaphore()

    @pl.loop(1, dests)
    def _(k):
        other = lax.rem(me + k, dests)
        pl.semaphore_signal(
            barrier, inc=1, device_id=(part, other), device_id_type=pl.DeviceIdType.MESH
        )

    pl.semaphore_wait(barrier, dests - 1)
    has_tail = quarter < QUART - 1
    no_lead = quarter >= QUART - 2
    stay = pltpu.make_async_copy(spec_ref.at[me, head], recv_ref.at[me, head], local.at[0])
    stay_tail = pltpu.make_async_copy(spec_ref.at[me, tail], recv_ref.at[me, tail], local.at[1])
    fill_table(high_ref, low_ref, table)

    @pl.when(has_tail)
    def _():
        for h in range(2):
            form(x_ref, fir_ref, table, filt, spec_ref, frames + parts[h][0], parts[h][1])

            @pl.loop(0, dests)
            def _(d):
                @pl.when(quarter < lax.div(d, groups) - 1)
                def _():
                    send_lead(d, h).start()

            @pl.loop(1, dests)
            def _(k):
                d = lax.rem(me + k, dests)

                @pl.when(no_lead | (quarter >= lax.div(d, groups)))
                def _():
                    send_tail(d, h).start()

        stay_tail.start()

    form(x_ref, fir_ref, table, filt, spec_ref, 0, frames)

    @pl.loop(1, dests)
    def _(k):
        d = lax.rem(me + k, dests)

        @pl.when(quarter >= lax.div(d, groups))
        def _():
            send_own(d).start()

    stay.start()

    @pl.loop(0, dests)
    def _(d):
        @pl.when(quarter < lax.div(d, groups) - 1)
        def _():
            send_lead(d, 0).wait_send()
            send_lead(d, 1).wait_send()

    @pl.loop(1, dests)
    def _(k):
        d = lax.rem(me + dests - k, dests)
        target = lax.div(d, groups)

        @pl.when((quarter == 0) & (target > 0))
        def _():
            send_own(d).start()

        @pl.when((quarter < QUART - 2) & (quarter == target - 1))
        def _():
            send_tail(d, 0).start()
            send_tail(d, 1).start()

    @pl.loop(0, dests)
    def _(d):
        @pl.when((quarter >= 1) & (quarter < lax.div(d, groups)))
        def _():
            send_lead(d, 0).wait_recv()
            send_lead(d, 1).wait_recv()

            @pl.loop(0, lead)
            def _(f):
                merged[d, f] = (
                    merged[d, f].astype(jnp.float32) + spec_ref[d, f].astype(jnp.float32)
                ).astype(jnp.bfloat16)

            for f in range(lead, frames):
                merged[d, f] = spec_ref[d, f]
            send_merged(d).start()

    stay.wait()
    pl.when(has_tail)(stay_tail.wait)

    @pl.loop(1, dests)
    def _(k):
        d = lax.rem(me + k, dests)
        target = lax.div(d, groups)
        send_own(d).wait_send()

        @pl.when(has_tail & (quarter >= target - 1))
        def _():
            send_tail(d, 0).wait_send()
            send_tail(d, 1).wait_send()

        remote(
            spec_ref.at[d, head], recv_ref.at[d, head], own_send.at[d], own_recv.at[d], d
        ).wait_recv()

        @pl.when((target < QUART - 1) & (target >= quarter - 1))
        def _():
            for h in range(2):
                here = pl.ds(frames + parts[h][0], parts[h][1])
                remote(
                    spec_ref.at[d, here],
                    recv_ref.at[d, here],
                    tail_send.at[h, d],
                    tail_recv.at[h, d],
                    d,
                ).wait_recv()


def exchange(own_frames, fir, high, low, dests):
    frames, slots, frame_len = own_frames.shape
    lead = fir.shape[0] - 1
    chans = low.shape[1]
    chan_dev = chans // dests
    spectra = (dests, frames + lead, 2, chan_dev, slots)
    copies = pltpu.SemaphoreType.DMA((dests,))
    return pl.pallas_call(
        exchange_kernel,
        out_shape=jax.ShapeDtypeStruct(spectra, jnp.bfloat16),
        in_specs=[pl.BlockSpec(memory_space=pltpu.VMEM)] * 4,
        out_specs=pl.BlockSpec(memory_space=pl.ANY),
        scratch_shapes=[
            pltpu.VMEM((2 * chans, frame_len), jnp.bfloat16),
            pltpu.VMEM((frames, slots, frame_len), jnp.bfloat16),
            pltpu.VMEM(spectra, jnp.bfloat16),
            pltpu.VMEM((dests, frames, 2, chan_dev, slots), jnp.bfloat16),
        ]
        + [copies] * 2
        + [pltpu.SemaphoreType.DMA((2, dests))] * 4
        + [pltpu.SemaphoreType.DMA((2,))],
        compiler_params=pltpu.CompilerParams(
            collective_id=0, has_side_effects=True, vmem_limit_bytes=VMEM
        ),
        name="exchange",
    )(own_frames, fir, high, low)


def correlate_kernel(spec_ref, order_ref, out_ref, gathered, select, ordered):
    sources, outs, _, chan_dev, slots = spec_ref.shape
    groups = sources // QUART
    inputs = order_ref.shape[0]
    rows_total = gathered.shape[0] // chan_dev
    frames = rows_total // (2 * QUART)
    lead = outs - frames
    spectra_total = QUART * frames

    quarter = lax.div(lax.axis_index("chan"), groups)

    def gather(q, add):
        for p in range(2):
            base = (p * QUART + q) * frames * chan_dev
            for g in range(groups):
                cols = slice(g * slots, (g + 1) * slots)
                source = q * groups + g
                for f in range(frames):
                    value = spec_ref[source, f, p]
                    if add and f < lead:
                        value = (
                            value.astype(jnp.float32)
                            + spec_ref[source - groups, frames + f, p].astype(jnp.float32)
                        ).astype(jnp.bfloat16)
                    gathered[base + f * chan_dev : base + (f + 1) * chan_dev, cols] = value

    @pl.when(pl.program_id(0) == 0)
    def _():
        gather(0, False)
        for q in range(1, QUART):
            pl.when(q >= quarter)(lambda q=q: gather(q, True))
            pl.when(q < quarter)(lambda q=q: gather(q, False))
        for begin in range(0, inputs, 128):
            names = lax.broadcasted_iota(jnp.int32, (128, inputs), 1)
            hit = names == order_ref[begin : begin + 128, :]
            select[begin : begin + 128, :] = hit.astype(jnp.float32).astype(jnp.bfloat16)

        @pl.loop(0, gathered.shape[0] // 256)
        def _(step):
            rows = pl.ds(pl.multiple_of(step * 256, 256), 256)
            result = jnp.dot(gathered[rows, :], select[...], preferred_element_type=jnp.float32)
            for k in range(inputs // 128):
                ordered[k, rows, :] = result[:, k * 128 : (k + 1) * 128]

    own_rows = pl.ds(pl.program_id(0), rows_total, stride=chan_dev)
    both = jnp.concatenate([ordered[k, own_rows, :] for k in range(inputs // 128)], axis=1)
    half = rows_total // 2
    turned = both.T.astype(jnp.bfloat16)
    auto_side = both.astype(jnp.bfloat16)
    cross_side = jnp.concatenate([both[half:], -both[:half]], axis=0).astype(jnp.bfloat16)
    tile = 256
    scale = 1.0 / spectra_total
    upper = lax.broadcasted_iota(jnp.int32, (tile, tile), 0) <= lax.broadcasted_iota(
        jnp.int32, (tile, tile), 1
    )
    for begin in range(0, inputs, tile):
        left = turned[begin : begin + tile]
        for other in range(0, inputs, tile):
            cols = slice(other, other + tile)
            value = None
            if other >= begin:
                value = jnp.dot(left, auto_side[:, cols], preferred_element_type=jnp.float32)
            if other <= begin:
                cross = jnp.dot(left, cross_side[:, cols], preferred_element_type=jnp.float32)
                value = cross if value is None else jnp.where(upper, value, cross)
            out_ref[0, begin : begin + tile, cols] = (value * scale).astype(jnp.bfloat16)


def correlate(received, input_order, frames):
    sources, outs, _, chan_dev, slots = received.shape
    inputs = input_order.shape[0]
    rows = 2 * QUART * frames * chan_dev
    return pl.pallas_call(
        correlate_kernel,
        grid=(chan_dev,),
        out_shape=jax.ShapeDtypeStruct((chan_dev, inputs, inputs), jnp.bfloat16),
        in_specs=[pl.BlockSpec(memory_space=pltpu.VMEM)] * 2,
        out_specs=pl.BlockSpec((1, inputs, inputs), lambda c: (c, 0, 0)),
        scratch_shapes=[
            pltpu.VMEM((rows, inputs), jnp.bfloat16),
            pltpu.VMEM((inputs, inputs), jnp.bfloat16),
            pltpu.VMEM((inputs // 128, rows, 128), jnp.float32),
        ],
        compiler_params=pltpu.CompilerParams(vmem_limit_bytes=VMEM),
        name="correlate",
    )(received, input_order[:, None])


def by_kernels(samples, fir, chan_assign, input_order):
    own_frames = samples[0]
    frames, _, frame_len = own_frames.shape
    chan_count = lax.axis_size("chan")
    high, low = phase_parts(chan_assign, frame_len)
    received = exchange(own_frames, fir, high, low, chan_count)
    return correlate(received, input_order, frames)


def plain(samples, fir, chan_assign, input_order):
    own_frames = samples[0]
    frames_quarter, slots_dev, frame_len = own_frames.shape
    taps_count = fir.shape[0]
    chan_count = lax.axis_size("chan")
    group_count = chan_count // QUART
    history_len = taps_count - 1
    lead_len = min(frames_quarter, history_len)
    tail_frames = own_frames[frames_quarter - lead_len :]
    pieces = shifted(tail_frames, "chan", 1 * group_count)
    extended = jnp.concatenate([pieces, own_frames], axis=0)
    dft_table = make_table(chan_assign, frame_len)
    chan_dev = chan_assign.shape[0] // chan_count
    inputs_all = input_order.shape[0]
    spectra_total = QUART * frames_quarter
    accum = jnp.zeros((frames_quarter, slots_dev, frame_len), jnp.float32)
    for tap_index in range(taps_count):
        begin = 0 + history_len - tap_index
        accum = accum + fir[tap_index][None, None, :] * extended[
            begin : begin + frames_quarter
        ].astype(jnp.float32)
    filtered = accum.astype(jnp.bfloat16)
    spectra = jnp.einsum("pcn,fin->cfpi", dft_table, filtered, preferred_element_type=jnp.float32)
    spectra = spectra.astype(jnp.bfloat16).reshape(
        chan_count, chan_dev, frames_quarter, 2, slots_dev
    )
    received = lax.all_to_all(spectra, "chan", split_axis=0, concat_axis=4, tiled=True)
    items = received.shape[1]
    row_count = received.shape[2]
    split_parts = received.reshape(items * row_count * 2 * QUART, inputs_all)
    select = (input_order[:, None] == jnp.arange(inputs_all, dtype=jnp.int32)[None, :]).astype(
        jnp.bfloat16
    )
    ordered = jnp.dot(split_parts, select, preferred_element_type=jnp.float32).astype(jnp.bfloat16)
    ordered = ordered.reshape(items, row_count, 2, QUART, inputs_all)
    stacked = ordered.reshape(items, row_count * 2 * QUART, inputs_all)
    real_rows = ordered[:, :, 0].reshape(items, row_count * QUART, inputs_all)
    imag_rows = ordered[:, :, 1].reshape(items, row_count * QUART, inputs_all)
    auto_sum = jnp.einsum("kra,krb->kab", stacked, stacked, preferred_element_type=jnp.float32)
    cross_sum = jnp.einsum("kra,krb->kab", real_rows, imag_rows, preferred_element_type=jnp.float32)
    row_index = lax.broadcasted_iota(jnp.int32, (inputs_all, inputs_all), 0)
    col_index = lax.broadcasted_iota(jnp.int32, (inputs_all, inputs_all), 1)
    upper_mask = (row_index <= col_index)[None, :, :]
    packed = (
        jnp.where(upper_mask, auto_sum, cross_sum - jnp.swapaxes(cross_sum, 1, 2)) / spectra_total
    )
    return packed.astype(jnp.bfloat16)


def on_device(samples, fir, chan_assign, input_order):
    _, frames, slots, frame_len = samples.shape
    chan_dev = chan_assign.shape[0] // lax.axis_size("chan")
    whole = slots % 256 == 0 and chan_dev % 16 == 0 and frame_len % 128 == 0
    whole = whole and fir.shape[0] - 1 <= frames and input_order.shape[0] % 256 == 0
    form = by_kernels if whole else plain
    return form(samples, fir, chan_assign, input_order)


def solution(mesh):
    in_specs = (P(("grp", "chan"), None, None, None), P(), P(), P())
    out_specs = P(("grp", "chan"), None, None)
    return jax.shard_map(
        on_device, mesh=mesh, in_specs=in_specs, out_specs=out_specs, check_vma=False
    )
```
